32 devices in a mesh: dp: 8 (over z, core), vocab: 4 (over y, x).
Axes of the slice: x: 2, y: 2, z: 4, core: 2. Of those that a mesh axis runs over, the one named last changes fastest.
Arguments:
- student_hidden: bfloat16 [48, 5120], P('dp', 'vocab'), may hold values from -71 to 71
- teacher_hidden: bfloat16 [48, 4096], P('dp', 'vocab'), may hold values from -73 to 73
- student_head: bfloat16 [5632, 5120], P(('dp', 'vocab')), may hold values from -16 to 16
- teacher_head: bfloat16 [5632, 4096], P(('dp', 'vocab')), may hold values from -16 to 16
Outputs:
- hidden_grad: bfloat16 [48, 5120], P('dp', 'vocab')
- head_grad: bfloat16 [5632, 5120], P(('dp', 'vocab'))
The draws below stay inside these ranges and needn't reach their ends.
All inputs are finite; a program needn't handle non-finite values.
Results may differ from the reference program's by a relative error of at most 0.017.
Values may be sent and summed in bfloat16 or wider, within the bound.
No kernel may reach another device: no remote copies, remote signals or barrier semaphores. Data moves between devices by JAX's collectives and lax.ppermute only.
A program may use at most 64 MiB of HBM per device.

```python
import math
import jax
import jax.numpy as jnp
from jax import lax

D = 5120
DT = 4096
VOC_DEV = 176
VOCAB = 5632
TOKENS = 48
DEVICES = 32


def head_matrix(key, marker, breadth, trended):
    seeded = jax.random.fold_in(key, marker)
    entry_key, scale_key = jax.random.split(seeded)
    rising = 1.0 + 2.0 * jnp.arange(VOCAB, dtype=jnp.float32) / VOCAB
    spread = jnp.exp(jax.random.uniform(scale_key, (VOCAB,), jnp.float32, math.log(0.5), math.log(1.0)))
    if trended:
        trend = rising
    else:
        trend = jnp.ones((VOCAB,), jnp.float32)
    entries = jax.random.normal(entry_key, (VOCAB, breadth), jnp.float32)
    matrix = entries * (spread * trend)[:, None] / math.sqrt(breadth)
    return jnp.clip(matrix, -16.0, 16.0)


def hidden_rows(key, marker, breadth):
    seeded = jax.random.fold_in(key, marker)
    normal_key = jax.random.fold_in(seeded, 0)
    samples = jax.random.normal(normal_key, (TOKENS, breadth), jnp.float32)
    limit = float(64 + 40000 // breadth)
    return jnp.clip(samples, -limit, limit)


def draw_student_head(key, part):
    return head_matrix(key, 11, D, False).astype(jnp.bfloat16)


def draw_teacher_head(key, part):
    return head_matrix(key, 12, DT, True).astype(jnp.bfloat16)


def draw_student_hidden(key, part):
    return hidden_rows(key, 21, D).astype(jnp.bfloat16)


def draw_teacher_hidden(key, part):
    return hidden_rows(key, 22, DT).astype(jnp.bfloat16)


def setup_inputs(seed: int = 0) -> dict:
    key_of = jax.random.split(jax.random.key(seed), 5)
    return {
        "student_hidden": draw_student_hidden(jax.random.fold_in(key_of[4], 71), 0),
        "teacher_hidden": draw_teacher_hidden(jax.random.fold_in(key_of[4], 71), 0),
        "student_head": draw_student_head(jax.random.fold_in(key_of[4], 71), 0),
        "teacher_head": draw_teacher_head(jax.random.fold_in(key_of[4], 71), 0),
    }


def log_total(logits):
    peak = lax.optimization_barrier(jnp.max(logits, axis=1, keepdims=True))
    return peak + jnp.log(lax.optimization_barrier(jnp.sum(jnp.exp(logits - peak), axis=1, keepdims=True)))

def reference(student_hidden, teacher_hidden, student_head, teacher_head):
    student_logits = lax.dot_general(student_hidden, student_head, (((1,), (1,)), ((), ())), preferred_element_type=jnp.float32)
    teacher_logits = lax.dot_general(teacher_hidden, teacher_head, (((1,), (1,)), ((), ())), preferred_element_type=jnp.float32)
    log_student = student_logits - log_total(student_logits)
    log_teacher = teacher_logits - log_total(teacher_logits)
    probs = jnp.exp(log_student)
    gap = log_student - log_teacher
    divergence = lax.optimization_barrier(jnp.sum(probs * gap, axis=1, keepdims=True))
    logit_grad = (probs * (gap - divergence)).astype(jnp.bfloat16)
    hidden_sum = jnp.dot(logit_grad, student_head, preferred_element_type=jnp.float32)
    grad_blocks = jnp.transpose(logit_grad.reshape(TOKENS, DEVICES, VOC_DEV), (1, 0, 2))

    def block_grad(block):
        product = lax.dot_general(block, student_hidden, (((0,), (0,)), ((), ())), preferred_element_type=jnp.float32)
        return product.astype(jnp.bfloat16)
    head_blocks = lax.map(block_grad, grad_blocks)
    head_sum = head_blocks.reshape(VOCAB, D)
    return (hidden_sum.astype(jnp.bfloat16), head_sum)
```

```python
import jax
import jax.numpy as jnp
from jax import lax
from jax.sharding import PartitionSpec as P


def doubled(value, axis, size, bits):
    me = lax.axis_index(axis)
    for bit in bits:
        pairs = [(i, i ^ (1 << bit)) for i in range(size)]
        other = lax.ppermute(value, axis, pairs)
        upper = (me >> bit) & 1
        value = jnp.where(
            upper == 1,
            jnp.concatenate([other, value], axis=0),
            jnp.concatenate([value, other], axis=0),
        )
    return value


def build(dp, vocab):
    dp_bits = dp.bit_length() - 1
    vocab_bits = vocab.bit_length() - 1

    def on_device(student_hidden, teacher_hidden, student_head, teacher_head):
        rows, share = student_hidden.shape
        teacher_share = teacher_hidden.shape[1]
        tokens = rows * dp
        packed = jnp.concatenate([student_hidden, teacher_hidden], axis=1)[None]
        by_z = doubled(packed, "dp", dp, range(1, dp_bits))
        by_vocab = doubled(by_z[None], "vocab", vocab, range(vocab_bits))
        by_core = doubled(by_vocab[None], "dp", dp, range(1))
        whole = jnp.transpose(by_core, (2, 0, 3, 1, 4))
        student_full = whole[..., :share].reshape(tokens, share * vocab)
        teacher_full = whole[..., share:].reshape(tokens, teacher_share * vocab)

        contract = (((1,), (1,)), ((), ()))
        student_logits = lax.dot_general(
            student_full, student_head, contract, preferred_element_type=jnp.float32
        )
        teacher_logits = lax.dot_general(
            teacher_full, teacher_head, contract, preferred_element_type=jnp.float32
        )
        peak = jnp.max(student_logits, axis=1)
        shifted = jnp.exp(student_logits - peak[:, None])
        total = jnp.sum(shifted, axis=1)
        weighted = jnp.sum(shifted * (student_logits - teacher_logits), axis=1)
        other_peak = jnp.max(teacher_logits, axis=1)
        other_total = jnp.sum(jnp.exp(teacher_logits - other_peak[:, None]), axis=1)
        stats = jnp.stack([peak, total, weighted, other_peak, other_total])
        devices = dp * vocab
        every = lax.all_to_all(
            jnp.broadcast_to(stats[None], (devices,) + stats.shape),
            ("dp", "vocab"), 0, 0, tiled=True,
        )
        top = jnp.max(every[:, 0], axis=0)
        scale = jnp.exp(every[:, 0] - top)
        total_all = jnp.sum(every[:, 1] * scale, axis=0)
        weighted_all = jnp.sum(every[:, 2] * scale, axis=0)
        other_top = jnp.max(every[:, 3], axis=0)
        other_all = jnp.sum(every[:, 4] * jnp.exp(every[:, 3] - other_top), axis=0)
        student_lse = (top + jnp.log(total_all))[:, None]
        teacher_lse = (other_top + jnp.log(other_all))[:, None]
        divergence = (weighted_all / total_all)[:, None] - student_lse + teacher_lse
        log_student = student_logits - student_lse
        probs = jnp.exp(log_student)
        gap = log_student - (teacher_logits - teacher_lse)
        logit_grad = (probs * (gap - divergence)).astype(jnp.bfloat16)

        partial = jnp.dot(
            logit_grad, student_head, preferred_element_type=jnp.float32
        ).astype(jnp.bfloat16)
        by_feature = jnp.transpose(partial.reshape(tokens, vocab, share), (1, 0, 2))
        arrived = lax.all_to_all(by_feature, "vocab", 0, 0, tiled=True)
        summed = jnp.sum(arrived.astype(jnp.float32), axis=0).astype(jnp.bfloat16)
        landed = lax.all_to_all(summed.reshape(dp, rows, share), "dp", 0, 0, tiled=True)
        hidden_grad = jnp.sum(landed.astype(jnp.float32), axis=0).astype(jnp.bfloat16)

        head_grad = lax.dot_general(
            logit_grad, student_full, (((0,), (0,)), ((), ())), preferred_element_type=jnp.float32
        ).astype(jnp.bfloat16)
        return (hidden_grad, head_grad)

    return on_device


def solution(mesh):
    return jax.shard_map(
        build(mesh.shape["dp"], mesh.shape["vocab"]),
        mesh=mesh,
        in_specs=(
            P("dp", "vocab"),
            P("dp", "vocab"),
            P(("dp", "vocab"), None),
            P(("dp", "vocab"), None),
        ),
        out_specs=(P("dp", "vocab"), P(("dp", "vocab"), None)),
        check_vma=False,
    )
```

```python
import jax
import jax.numpy as jnp
from jax import lax
from jax.sharding import PartitionSpec as P


def grouped(bits):
    bits = list(bits)
    return [bits[i : i + 2] for i in range(0, len(bits), 2)]


def mask_of(j, bits):
    return sum(((j >> k) & 1) << bit for k, bit in enumerate(bits))


def reorder(parts, index, bits):
    for k, bit in enumerate(bits):
        upper = ((index >> bit) & 1) == 1
        parts = [jnp.where(upper, parts[j ^ (1 << k)], parts[j]) for j in range(len(parts))]
    return parts


def swap(value, axis, size, mask):
    return lax.ppermute(value, axis, [(i, i ^ mask) for i in range(size)])


def gathered(value, axis, size, bits, dim):
    index = lax.axis_index(axis)
    for group in grouped(bits):
        parts = [value] + [
            swap(value, axis, size, mask_of(j, group)) for j in range(1, 1 << len(group))
        ]
        value = jnp.concatenate(reorder(parts, index, group), axis=dim)
    return value


def scattered(total, axis, size, bits, dim):
    index = lax.axis_index(axis)
    for group in reversed(grouped(bits)):
        parts = reorder(jnp.split(total, 1 << len(group), axis=dim), index, group)
        total = parts[0]
        landed = [
            swap(parts[j].astype(jnp.bfloat16), axis, size, mask_of(j, group))
            for j in range(1, 1 << len(group))
        ]
        for part in landed:
            total = total + part.astype(jnp.float32)
    return total


def build(dp, vocab):
    dp_bits = range(dp.bit_length() - 1)
    vocab_bits = range(vocab.bit_length() - 1)
    core, z_bits = dp_bits[:1], dp_bits[1:]

    def on_device(student_hidden, teacher_hidden, student_head, teacher_head):
        rows, share = student_hidden.shape
        packed = jnp.concatenate([student_hidden, teacher_hidden], axis=1)
        by_z = gathered(packed, "dp", dp, z_bits, 0)
        by_vocab = gathered(by_z[None], "vocab", vocab, vocab_bits, 0)
        whole = gathered(by_vocab, "dp", dp, core, 1)
        student_full = jnp.concatenate([whole[i, :, :share] for i in range(vocab)], axis=1)
        teacher_full = jnp.concatenate([whole[i, :, share:] for i in range(vocab)], axis=1)

        contract = (((1,), (1,)), ((), ()))
        student_logits = lax.dot_general(
            student_full, student_head, contract, preferred_element_type=jnp.float32
        )
        teacher_logits = lax.dot_general(
            teacher_full, teacher_head, contract, preferred_element_type=jnp.float32
        )
        peak = jnp.max(student_logits, axis=1)
        shifted = jnp.exp(student_logits - peak[:, None])
        total = jnp.sum(shifted, axis=1)
        weighted = jnp.sum(shifted * (student_logits - teacher_logits), axis=1)
        other_peak = jnp.max(teacher_logits, axis=1)
        other_total = jnp.sum(jnp.exp(teacher_logits - other_peak[:, None]), axis=1)
        stats = jnp.stack([peak, total, weighted, other_peak, other_total])
        devices = dp * vocab
        every = lax.all_to_all(
            jnp.broadcast_to(stats[None], (devices,) + stats.shape),
            ("dp", "vocab"), 0, 0, tiled=True,
        )
        top = jnp.max(every[:, 0], axis=0)
        scale = jnp.exp(every[:, 0] - top)
        total_all = jnp.sum(every[:, 1] * scale, axis=0)
        weighted_all = jnp.sum(every[:, 2] * scale, axis=0)
        other_top = jnp.max(every[:, 3], axis=0)
        other_all = jnp.sum(every[:, 4] * jnp.exp(every[:, 3] - other_top), axis=0)
        student_lse = (top + jnp.log(total_all))[:, None]
        teacher_lse = (other_top + jnp.log(other_all))[:, None]
        divergence = (weighted_all / total_all)[:, None] - student_lse + teacher_lse
        log_student = student_logits - student_lse
        probs = jnp.exp(log_student)
        gap = log_student - (teacher_logits - teacher_lse)
        logit_grad = (probs * (gap - divergence)).astype(jnp.bfloat16)

        index = lax.axis_index("dp")
        half = logit_grad.shape[0] // 2
        keep, send = reorder([logit_grad[:half], logit_grad[half:]], index, core)
        away = jnp.dot(send, student_head, preferred_element_type=jnp.float32).astype(jnp.bfloat16)
        landed = swap(away, "dp", dp, 1)
        acc = jnp.dot(keep, student_head, preferred_element_type=jnp.float32)
        acc = acc + landed.astype(jnp.float32)
        acc = scattered(acc, "vocab", vocab, vocab_bits, 1)
        acc = scattered(acc, "dp", dp, z_bits, 0)
        hidden_grad = acc.astype(jnp.bfloat16)

        head_grad = lax.dot_general(
            logit_grad, student_full, (((0,), (0,)), ((), ())), preferred_element_type=jnp.float32
        ).astype(jnp.bfloat16)
        return (hidden_grad, head_grad)

    return on_device


def solution(mesh):
    return jax.shard_map(
        build(mesh.shape["dp"], mesh.shape["vocab"]),
        mesh=mesh,
        in_specs=(
            P("dp", "vocab"),
            P("dp", "vocab"),
            P(("dp", "vocab"), None),
            P(("dp", "vocab"), None),
        ),
        out_specs=(P("dp", "vocab"), P(("dp", "vocab"), None)),
        check_vma=False,
    )
```

```python
import jax
import jax.numpy as jnp
from jax import lax
from jax.sharding import PartitionSpec as P


def grouped(bits):
    bits = list(bits)
    return [bits[i : i + 2] for i in range(0, len(bits), 2)]


def mask_of(j, bits):
    return sum(((j >> k) & 1) << bit for k, bit in enumerate(bits))


def reorder(parts, index, bits):
    for k, bit in enumerate(bits):
        upper = ((index >> bit) & 1) == 1
        parts = [jnp.where(upper, parts[j ^ (1 << k)], parts[j]) for j in range(len(parts))]
    return parts


def swap(value, axis, size, mask):
    return lax.ppermute(value, axis, [(i, i ^ mask) for i in range(size)])


def gathered(value, axis, size, bits, dim):
    index = lax.axis_index(axis)
    for group in grouped(bits):
        parts = [value] + [
            swap(value, axis, size, mask_of(j, group)) for j in range(1, 1 << len(group))
        ]
        value = jnp.concatenate(reorder(parts, index, group), axis=dim)
    return value


def build(dp, vocab):
    dp_bits = range(dp.bit_length() - 1)
    vocab_bits = range(vocab.bit_length() - 1)
    core, z_bits = dp_bits[:1], dp_bits[1:]

    def on_device(student_hidden, teacher_hidden, student_head, teacher_head):
        rows, share = student_hidden.shape
        teacher_share = teacher_hidden.shape[1]
        tokens = rows * dp
        packed = jnp.concatenate([student_hidden, teacher_hidden], axis=1)[None]
        by_z = gathered(packed, "dp", dp, z_bits, 0)
        by_z = by_z.reshape(1, tokens // 2, share + teacher_share)
        by_vocab = gathered(by_z, "vocab", vocab, vocab_bits, 0)
        whole = gathered(by_vocab, "dp", dp, core, 1)
        student_full = jnp.concatenate([whole[i, :, :share] for i in range(vocab)], axis=1)
        teacher_full = jnp.concatenate([whole[i, :, share:] for i in range(vocab)], axis=1)

        contract = (((1,), (1,)), ((), ()))
        student_logits = lax.dot_general(
            student_full, student_head, contract, preferred_element_type=jnp.float32
        )
        teacher_logits = lax.dot_general(
            teacher_full, teacher_head, contract, preferred_element_type=jnp.float32
        )
        peak = jnp.max(student_logits, axis=1)
        shifted = jnp.exp(student_logits - peak[:, None])
        total = jnp.sum(shifted, axis=1)
        weighted = jnp.sum(shifted * (student_logits - teacher_logits), axis=1)
        other_peak = jnp.max(teacher_logits, axis=1)
        other_total = jnp.sum(jnp.exp(teacher_logits - other_peak[:, None]), axis=1)
        stats = jnp.stack([peak, total, weighted, other_peak, other_total])
        stats = jnp.pad(stats, ((0, 3), (0, -tokens % 128)))
        devices = dp * vocab
        every = lax.all_to_all(
            jnp.broadcast_to(stats[None], (devices,) + stats.shape),
            ("dp", "vocab"), 0, 0, tiled=True,
        )[:, :, :tokens]
        top = jnp.max(every[:, 0], axis=0)
        scale = jnp.exp(every[:, 0] - top)
        total_all = jnp.sum(every[:, 1] * scale, axis=0)
        weighted_all = jnp.sum(every[:, 2] * scale, axis=0)
        other_top = jnp.max(every[:, 3], axis=0)
        other_all = jnp.sum(every[:, 4] * jnp.exp(every[:, 3] - other_top), axis=0)
        student_lse = (top + jnp.log(total_all))[:, None]
        teacher_lse = (other_top + jnp.log(other_all))[:, None]
        divergence = (weighted_all / total_all)[:, None] - student_lse + teacher_lse
        log_student = student_logits - student_lse
        probs = jnp.exp(log_student)
        gap = log_student - (teacher_logits - teacher_lse)
        logit_grad = (probs * (gap - divergence)).astype(jnp.bfloat16)

        index = lax.axis_index("dp")
        half = logit_grad.shape[0] // 2
        keep, send = reorder([logit_grad[:half], logit_grad[half:]], index, core)
        away = jnp.dot(send, student_head, preferred_element_type=jnp.float32).astype(jnp.bfloat16)
        landed = swap(away, "dp", dp, 1)
        acc = jnp.dot(keep, student_head, preferred_element_type=jnp.float32)
        acc = acc + landed.astype(jnp.float32)
        zs = dp // 2
        blocks = acc.astype(jnp.bfloat16).reshape(zs, rows, vocab, share)
        blocks = jnp.transpose(blocks, (0, 2, 1, 3)).reshape(zs * vocab, rows, share)
        groups = [
            [(z * 2 + c) * vocab + v for z in range(zs) for v in range(vocab)] for c in range(2)
        ]
        landed = lax.all_to_all(
            blocks, ("dp", "vocab"), 0, 0, axis_index_groups=groups, tiled=True
        )
        hidden_grad = jnp.sum(landed.astype(jnp.float32), axis=0).astype(jnp.bfloat16)

        head_grad = lax.dot_general(
            logit_grad, student_full, (((0,), (0,)), ((), ())), preferred_element_type=jnp.float32
        ).astype(jnp.bfloat16)
        return (hidden_grad, head_grad)

    return on_device


def solution(mesh):
    return jax.shard_map(
        build(mesh.shape["dp"], mesh.shape["vocab"]),
        mesh=mesh,
        in_specs=(
            P("dp", "vocab"),
            P("dp", "vocab"),
            P(("dp", "vocab"), None),
            P(("dp", "vocab"), None),
        ),
        out_specs=(P("dp", "vocab"), P(("dp", "vocab"), None)),
        check_vma=False,
    )
```

```python
import jax
import jax.numpy as jnp
from jax import lax
from jax.sharding import PartitionSpec as P


def grouped(bits):
    bits = list(bits)
    return [bits[i : i + 2] for i in range(0, len(bits), 2)]


def mask_of(j, bits):
    return sum(((j >> k) & 1) << bit for k, bit in enumerate(bits))


def reorder(parts, index, bits):
    for k, bit in enumerate(bits):
        lower = ((index >> bit) & 1) == 0
        parts = [jnp.where(lower, parts[j], parts[j ^ (1 << k)]) for j in range(len(parts))]
    return parts


def swap(value, axis, size, mask):
    return lax.ppermute(value, axis, [(i, i ^ mask) for i in range(size)])


def gathered(value, axis, size, bits, dim):
    index = lax.axis_index(axis)
    for group in grouped(bits):
        landed = {
            j: swap(value, axis, size, mask_of(j, group))
            for j in reversed(range(1, 1 << len(group)))
        }
        parts = [value] + [landed[j] for j in range(1, 1 << len(group))]
        value = jnp.concatenate(reorder(parts, index, group), axis=dim)
    return value


def scattered(total, axis, size, bits, dim):
    index = lax.axis_index(axis)
    for group in reversed(grouped(bits)):
        parts = reorder(jnp.split(total, 1 << len(group), axis=dim), index, group)
        total = parts[0]
        landed = [
            swap(parts[j].astype(jnp.bfloat16), axis, size, mask_of(j, group))
            for j in reversed(range(1, 1 << len(group)))
        ]
        for part in landed:
            total = total + part.astype(jnp.float32)
    return total


def build(dp, vocab):
    dp_bits = range(dp.bit_length() - 1)
    vocab_bits = range(vocab.bit_length() - 1)
    core, z_bits = dp_bits[:1], dp_bits[1:]

    def on_device(student_hidden, teacher_hidden, student_head, teacher_head):
        rows, share = student_hidden.shape
        teacher_share = teacher_hidden.shape[1]
        tokens = rows * dp
        lane = lax.broadcasted_iota(jnp.int32, (rows, share + teacher_share), 1)
        packed = jnp.where(
            lane < share,
            jnp.pad(student_hidden, ((0, 0), (0, teacher_share))),
            jnp.pad(teacher_hidden, ((0, 0), (share, 0))),
        )
        by_z = gathered(packed, "dp", dp, z_bits, 0)
        by_vocab = gathered(by_z[None], "vocab", vocab, vocab_bits, 0)
        whole = gathered(by_vocab, "dp", dp, core, 1)
        student_full = jnp.concatenate([whole[i, :, :share] for i in range(vocab)], axis=1)
        teacher_full = jnp.concatenate([whole[i, :, share:] for i in range(vocab)], axis=1)

        contract = (((1,), (1,)), ((), ()))
        student_logits = lax.dot_general(
            student_full, student_head, contract, preferred_element_type=jnp.float32
        )
        teacher_logits = lax.dot_general(
            teacher_full, teacher_head, contract, preferred_element_type=jnp.float32
        )
        peak = jnp.max(student_logits, axis=1)
        shifted = jnp.exp(student_logits - peak[:, None])
        total = jnp.sum(shifted, axis=1)
        weighted = jnp.sum(shifted * (student_logits - teacher_logits), axis=1)
        other_peak = jnp.max(teacher_logits, axis=1)
        other_total = jnp.sum(jnp.exp(teacher_logits - other_peak[:, None]), axis=1)
        lanes = -(-tokens // 64) * 64
        stats = jnp.stack([
            peak + jnp.log(total),
            weighted / total,
            other_peak + jnp.log(other_total),
            jnp.zeros_like(peak),
        ])
        stats = jnp.pad(stats, ((0, 0), (0, lanes - tokens))).reshape(2, 2 * lanes)
        devices = dp * vocab
        every = lax.all_to_all(
            jnp.broadcast_to(stats[None], (devices,) + stats.shape),
            ("dp", "vocab"), 0, 0, tiled=True,
        )
        each_lse = every[:, 0, :tokens]
        each_mean = every[:, 0, lanes : lanes + tokens]
        each_other = every[:, 1, :tokens]

        def joined(each):
            top = jnp.max(each, axis=0)
            return top + jnp.log(jnp.sum(jnp.exp(each - top), axis=0))

        student_lse = joined(each_lse)
        teacher_lse = joined(each_other)[:, None]
        mean = jnp.sum(jnp.exp(each_lse - student_lse) * each_mean, axis=0)[:, None]
        student_lse = student_lse[:, None]
        divergence = mean - student_lse + teacher_lse
        log_student = student_logits - student_lse
        probs = jnp.exp(log_student)
        gap = log_student - (teacher_logits - teacher_lse)
        logit_grad = (probs * (gap - divergence)).astype(jnp.bfloat16)

        index = lax.axis_index("dp")
        half = logit_grad.shape[0] // 2
        keep, send = reorder([logit_grad[:half], logit_grad[half:]], index, core)
        away = jnp.dot(send, student_head, preferred_element_type=jnp.float32).astype(jnp.bfloat16)
        landed = swap(away, "dp", dp, 1)
        near = lax.optimization_barrier(
            jnp.dot(keep, student_head, preferred_element_type=jnp.float32)
        )
        acc = near + landed.astype(jnp.float32)
        head_grad = lax.dot_general(
            logit_grad, student_full, (((0,), (0,)), ((), ())), preferred_element_type=jnp.float32
        ).astype(jnp.bfloat16)
        acc = scattered(acc, "vocab", vocab, vocab_bits, 1)
        acc, head_grad = lax.optimization_barrier((acc, head_grad))
        acc = scattered(acc, "dp", dp, z_bits, 0)
        hidden_grad = acc.astype(jnp.bfloat16)
        return (hidden_grad, head_grad)

    return on_device


def solution(mesh):
    return jax.shard_map(
        build(mesh.shape["dp"], mesh.shape["vocab"]),
        mesh=mesh,
        in_specs=(
            P("dp", "vocab"),
            P("dp", "vocab"),
            P(("dp", "vocab"), None),
            P(("dp", "vocab"), None),
        ),
        out_specs=(P("dp", "vocab"), P(("dp", "vocab"), None)),
        check_vma=False,
    )
```

```python
import jax
import jax.numpy as jnp
from jax import lax
from jax.sharding import PartitionSpec as P


def grouped(bits):
    bits = list(bits)
    return [bits[i : i + 2] for i in range(0, len(bits), 2)]


def mask_of(j, bits):
    return sum(((j >> k) & 1) << bit for k, bit in enumerate(bits))


def reorder(parts, index, bits):
    for k, bit in enumerate(bits):
        lower = ((index >> bit) & 1) == 0
        parts = [jnp.where(lower, parts[j], parts[j ^ (1 << k)]) for j in range(len(parts))]
    return parts


def swap(value, axis, size, mask):
    return lax.ppermute(value, axis, [(i, i ^ mask) for i in range(size)])


def gathered(value, axis, size, bits, dim):
    index = lax.axis_index(axis)
    for group in grouped(bits):
        landed = {
            j: swap(value, axis, size, mask_of(j, group))
            for j in reversed(range(1, 1 << len(group)))
        }
        parts = [value] + [landed[j] for j in range(1, 1 << len(group))]
        value = jnp.concatenate(reorder(parts, index, group), axis=dim)
    return value


def scattered(total, axis, size, bits, dim):
    index = lax.axis_index(axis)
    for group in reversed(grouped(bits)):
        parts = reorder(jnp.split(total, 1 << len(group), axis=dim), index, group)
        total = parts[0]
        landed = [
            swap(parts[j].astype(jnp.bfloat16), axis, size, mask_of(j, group))
            for j in reversed(range(1, 1 << len(group)))
        ]
        for part in landed:
            total = total + part.astype(jnp.float32)
    return total


def build(dp, vocab):
    dp_bits = range(dp.bit_length() - 1)
    vocab_bits = range(vocab.bit_length() - 1)
    core, z_bits = dp_bits[:1], dp_bits[1:]

    def on_device(student_hidden, teacher_hidden, student_head, teacher_head):
        rows, share = student_hidden.shape
        teacher_share = teacher_hidden.shape[1]
        tokens = rows * dp
        lane = lax.broadcasted_iota(jnp.int32, (rows, share + teacher_share), 1)
        packed = jnp.where(
            lane < share,
            jnp.pad(student_hidden, ((0, 0), (0, teacher_share))),
            jnp.pad(teacher_hidden, ((0, 0), (share, 0))),
        )
        by_z = gathered(packed, "dp", dp, z_bits, 0)
        by_vocab = gathered(by_z[None], "vocab", vocab, vocab_bits, 0)
        index = lax.axis_index("dp")
        teacher_half = jnp.concatenate([by_vocab[i, :, share:] for i in range(vocab)], axis=1)
        student_half = jnp.concatenate([by_vocab[i, :, :share] for i in range(vocab)], axis=1)
        teacher_full, student_full = [
            jnp.concatenate(reorder([rows_of_half, swap(rows_of_half, "dp", dp, 1)], index, core))
            for rows_of_half in (teacher_half, student_half)
        ]

        contract = (((1,), (1,)), ((), ()))
        student_logits = lax.dot_general(
            student_full, student_head, contract, preferred_element_type=jnp.float32
        )
        teacher_logits = lax.dot_general(
            teacher_full, teacher_head, contract, preferred_element_type=jnp.float32
        )
        peak = jnp.max(student_logits, axis=1)
        shifted = jnp.exp(student_logits - peak[:, None])
        total = jnp.sum(shifted, axis=1)
        weighted = jnp.sum(shifted * (student_logits - teacher_logits), axis=1)
        other_peak = jnp.max(teacher_logits, axis=1)
        other_total = jnp.sum(jnp.exp(teacher_logits - other_peak[:, None]), axis=1)
        lanes = -(-tokens // 64) * 64
        stats = jnp.stack([
            peak + jnp.log(total),
            weighted / total,
            other_peak + jnp.log(other_total),
            jnp.zeros_like(peak),
        ])
        stats = jnp.pad(stats, ((0, 0), (0, lanes - tokens))).reshape(2, 2 * lanes)
        devices = dp * vocab
        every = lax.all_to_all(
            jnp.broadcast_to(stats[None], (devices,) + stats.shape),
            ("dp", "vocab"), 0, 0, tiled=True,
        )
        each_lse = every[:, 0, :tokens]
        each_mean = every[:, 0, lanes : lanes + tokens]
        each_other = every[:, 1, :tokens]

        def joined(each):
            top = jnp.max(each, axis=0)
            return top + jnp.log(jnp.sum(jnp.exp(each - top), axis=0))

        student_lse = joined(each_lse)
        teacher_lse = joined(each_other)[:, None]
        mean = jnp.sum(jnp.exp(each_lse - student_lse) * each_mean, axis=0)[:, None]
        student_lse = student_lse[:, None]
        divergence = mean - student_lse + teacher_lse
        log_student = student_logits - student_lse
        probs = jnp.exp(log_student)
        gap = log_student - (teacher_logits - teacher_lse)
        logit_grad = (probs * (gap - divergence)).astype(jnp.bfloat16)

        half = logit_grad.shape[0] // 2
        keep, send = reorder([logit_grad[:half], logit_grad[half:]], index, core)
        away = jnp.dot(send, student_head, preferred_element_type=jnp.float32).astype(jnp.bfloat16)
        landed = swap(away, "dp", dp, 1)
        near = lax.optimization_barrier(
            jnp.dot(keep, student_head, preferred_element_type=jnp.float32)
        )
        acc = near + landed.astype(jnp.float32)
        head_grad = lax.dot_general(
            logit_grad, student_full, (((0,), (0,)), ((), ())), preferred_element_type=jnp.float32
        ).astype(jnp.bfloat16)
        acc = scattered(acc, "vocab", vocab, vocab_bits, 1)
        acc, head_grad = lax.optimization_barrier((acc, head_grad))
        acc = scattered(acc, "dp", dp, z_bits, 0)
        hidden_grad = acc.astype(jnp.bfloat16)
        return (hidden_grad, head_grad)

    return on_device


def solution(mesh):
    return jax.shard_map(
        build(mesh.shape["dp"], mesh.shape["vocab"]),
        mesh=mesh,
        in_specs=(
            P("dp", "vocab"),
            P("dp", "vocab"),
            P(("dp", "vocab"), None),
            P(("dp", "vocab"), None),
        ),
        out_specs=(P("dp", "vocab"), P(("dp", "vocab"), None)),
        check_vma=False,
    )
```

```python
import jax
import jax.numpy as jnp
from jax import lax
from jax.sharding import PartitionSpec as P


def grouped(bits):
    bits = list(bits)
    return [bits[i : i + 2] for i in range(0, len(bits), 2)]


def mask_of(j, bits):
    return sum(((j >> k) & 1) << bit for k, bit in enumerate(bits))


def reorder(parts, index, bits):
    for k, bit in enumerate(bits):
        lower = ((index >> bit) & 1) == 0
        parts = [jnp.where(lower, parts[j], parts[j ^ (1 << k)]) for j in range(len(parts))]
    return parts


def swap(value, axis, size, mask):
    return lax.ppermute(value, axis, [(i, i ^ mask) for i in range(size)])


def gathered(value, axis, size, bits, dim):
    index = lax.axis_index(axis)
    for group in grouped(bits):
        landed = {
            j: swap(value, axis, size, mask_of(j, group))
            for j in reversed(range(1, 1 << len(group)))
        }
        parts = lax.optimization_barrier([landed[j] for j in range(1, 1 << len(group))])
        parts = [value] + list(parts)
        value = jnp.concatenate(reorder(parts, index, group), axis=dim)
    return value


def scattered(total, axis, size, bits, dim):
    index = lax.axis_index(axis)
    for group in reversed(grouped(bits)):
        parts = reorder(jnp.split(total, 1 << len(group), axis=dim), index, group)
        total = parts[0]
        landed = [
            swap(parts[j].astype(jnp.bfloat16), axis, size, mask_of(j, group))
            for j in reversed(range(1, 1 << len(group)))
        ]
        for part in landed:
            total = total + part.astype(jnp.float32)
    return total


def build(dp, vocab):
    dp_bits = range(dp.bit_length() - 1)
    vocab_bits = range(vocab.bit_length() - 1)
    core, z_bits = dp_bits[:1], dp_bits[1:]

    def on_device(student_hidden, teacher_hidden, student_head, teacher_head):
        rows, share = student_hidden.shape
        teacher_share = teacher_hidden.shape[1]
        tokens = rows * dp
        lane = lax.broadcasted_iota(jnp.int32, (rows, share + teacher_share), 1)
        packed = jnp.where(
            lane < share,
            jnp.pad(student_hidden, ((0, 0), (0, teacher_share))),
            jnp.pad(teacher_hidden, ((0, 0), (share, 0))),
        )
        by_z = gathered(packed, "dp", dp, z_bits, 0)
        by_vocab = gathered(by_z[None], "vocab", vocab, vocab_bits, 0)
        whole = gathered(by_vocab, "dp", dp, core, 1)
        student_full = jnp.concatenate([whole[i, :, :share] for i in range(vocab)], axis=1)
        teacher_full = jnp.concatenate([whole[i, :, share:] for i in range(vocab)], axis=1)

        contract = (((1,), (1,)), ((), ()))
        student_logits = lax.dot_general(
            student_full, student_head, contract, preferred_element_type=jnp.float32
        )
        teacher_logits = lax.dot_general(
            teacher_full, teacher_head, contract, preferred_element_type=jnp.float32
        )
        peak = jnp.max(student_logits, axis=1)
        shifted = jnp.exp(student_logits - peak[:, None])
        total = jnp.sum(shifted, axis=1)
        weighted = jnp.sum(shifted * (student_logits - teacher_logits), axis=1)
        other_peak = jnp.max(teacher_logits, axis=1)
        other_total = jnp.sum(jnp.exp(teacher_logits - other_peak[:, None]), axis=1)
        lanes = -(-tokens // 64) * 64
        stats = jnp.stack([
            peak,
            total,
            weighted / total,
            other_peak + jnp.log(other_total),
        ])
        stats = jnp.pad(stats, ((0, 0), (0, lanes - tokens))).reshape(2, 2 * lanes)
        devices = dp * vocab
        every = lax.all_to_all(
            jnp.broadcast_to(stats[None], (devices,) + stats.shape),
            ("dp", "vocab"), 0, 0, tiled=True,
        )
        each_peak = every[:, 0, :tokens]
        each_total = every[:, 0, lanes : lanes + tokens]
        each_mean = every[:, 1, :tokens]
        each_other = every[:, 1, lanes : lanes + tokens]
        top = jnp.max(each_peak, axis=0)
        each_total = each_total * jnp.exp(each_peak - top)
        total_all = jnp.sum(each_total, axis=0)
        mean = (jnp.sum(each_total * each_mean, axis=0) / total_all)[:, None]
        student_lse = (top + jnp.log(total_all))[:, None]
        other_top = jnp.max(each_other, axis=0)
        other_all = jnp.sum(jnp.exp(each_other - other_top), axis=0)
        teacher_lse = (other_top + jnp.log(other_all))[:, None]
        divergence = mean - student_lse + teacher_lse
        log_student = student_logits - student_lse
        probs = jnp.exp(log_student)
        gap = log_student - (teacher_logits - teacher_lse)
        logit_grad = (probs * (gap - divergence)).astype(jnp.bfloat16)

        index = lax.axis_index("dp")
        half = logit_grad.shape[0] // 2
        keep, send = reorder([logit_grad[:half], logit_grad[half:]], index, core)
        away = jnp.dot(send, student_head, preferred_element_type=jnp.float32).astype(jnp.bfloat16)
        landed = swap(away, "dp", dp, 1)
        near = lax.optimization_barrier(
            jnp.dot(keep, student_head, preferred_element_type=jnp.float32)
        )
        acc = near + landed.astype(jnp.float32)
        head_grad = lax.dot_general(
            logit_grad, student_full, (((0,), (0,)), ((), ())), preferred_element_type=jnp.float32
        ).astype(jnp.bfloat16)
        acc = scattered(acc, "vocab", vocab, vocab_bits, 1)
        acc, head_grad = lax.optimization_barrier((acc, head_grad))
        acc = scattered(acc, "dp", dp, z_bits, 0)
        hidden_grad = acc.astype(jnp.bfloat16)
        return (hidden_grad, head_grad)

    return on_device


def solution(mesh):
    return jax.shard_map(
        build(mesh.shape["dp"], mesh.shape["vocab"]),
        mesh=mesh,
        in_specs=(
            P("dp", "vocab"),
            P("dp", "vocab"),
            P(("dp", "vocab"), None),
            P(("dp", "vocab"), None),
        ),
        out_specs=(P("dp", "vocab"), P(("dp", "vocab"), None)),
        check_vma=False,
    )
```

```python
import jax
import jax.numpy as jnp
from jax import lax
from jax.sharding import PartitionSpec as P


def grouped(bits):
    bits = list(bits)
    return [bits[i : i + 2] for i in range(0, len(bits), 2)]


def mask_of(j, bits):
    return sum(((j >> k) & 1) << bit for k, bit in enumerate(bits))


def reorder(parts, index, bits):
    for k, bit in enumerate(bits):
        lower = ((index >> bit) & 1) == 0
        parts = [jnp.where(lower, parts[j], parts[j ^ (1 << k)]) for j in range(len(parts))]
    return parts


def swap(value, axis, size, mask):
    return lax.ppermute(value, axis, [(i, i ^ mask) for i in range(size)])


def gathered(value, axis, size, bits, dim):
    index = lax.axis_index(axis)
    for group in grouped(bits):
        landed = {
            j: swap(value, axis, size, mask_of(j, group))
            for j in reversed(range(1, 1 << len(group)))
        }
        parts = lax.optimization_barrier([landed[j] for j in range(1, 1 << len(group))])
        parts = [value] + list(parts)
        value = jnp.concatenate(reorder(parts, index, group), axis=dim)
    return value


def scattered(total, axis, size, bits, dim, farthest_first=True):
    index = lax.axis_index(axis)
    for group in reversed(grouped(bits)):
        parts = reorder(jnp.split(total, 1 << len(group), axis=dim), index, group)
        total = parts[0]
        landed = [
            swap(parts[j].astype(jnp.bfloat16), axis, size, mask_of(j, group))
            for j in sorted(range(1, 1 << len(group)), reverse=farthest_first)
        ]
        for part in landed:
            total = total + part.astype(jnp.float32)
    return total


def build(dp, vocab):
    dp_bits = range(dp.bit_length() - 1)
    vocab_bits = range(vocab.bit_length() - 1)
    core, z_bits = dp_bits[:1], dp_bits[1:]

    def on_device(student_hidden, teacher_hidden, student_head, teacher_head):
        rows, share = student_hidden.shape
        teacher_share = teacher_hidden.shape[1]
        tokens = rows * dp
        lane = lax.broadcasted_iota(jnp.int32, (rows, share + teacher_share), 1)
        packed = jnp.where(
            lane < share,
            jnp.pad(student_hidden, ((0, 0), (0, teacher_share))),
            jnp.pad(teacher_hidden, ((0, 0), (share, 0))),
        )
        by_z = gathered(packed, "dp", dp, z_bits, 0)
        by_vocab = gathered(by_z[None], "vocab", vocab, vocab_bits, 0)
        whole = gathered(by_vocab, "dp", dp, core, 1)
        student_full = jnp.concatenate([whole[i, :, :share] for i in range(vocab)], axis=1)
        teacher_full = jnp.concatenate([whole[i, :, share:] for i in range(vocab)], axis=1)

        contract = (((1,), (1,)), ((), ()))
        student_logits = lax.dot_general(
            student_full, student_head, contract, preferred_element_type=jnp.float32
        )
        teacher_logits = lax.dot_general(
            teacher_full, teacher_head, contract, preferred_element_type=jnp.float32
        )
        peak = jnp.max(student_logits, axis=1)
        shifted = jnp.exp(student_logits - peak[:, None])
        total = jnp.sum(shifted, axis=1)
        weighted = jnp.sum(shifted * (student_logits - teacher_logits), axis=1)
        other_peak = jnp.max(teacher_logits, axis=1)
        other_total = jnp.sum(jnp.exp(teacher_logits - other_peak[:, None]), axis=1)
        lanes = -(-tokens // 64) * 64
        stats = jnp.stack([
            peak,
            total,
            weighted / total,
            other_peak + jnp.log(other_total),
        ])
        stats = jnp.pad(stats, ((0, 0), (0, lanes - tokens))).reshape(2, 2 * lanes)
        devices = dp * vocab
        every = lax.all_to_all(
            jnp.broadcast_to(stats[None], (devices,) + stats.shape),
            ("dp", "vocab"), 0, 0, tiled=True,
        )
        each_peak = every[:, 0, :tokens]
        each_total = every[:, 0, lanes : lanes + tokens]
        each_mean = every[:, 1, :tokens]
        each_other = every[:, 1, lanes : lanes + tokens]
        top = jnp.max(each_peak, axis=0)
        each_total = each_total * jnp.exp(each_peak - top)
        total_all = jnp.sum(each_total, axis=0)
        mean = (jnp.sum(each_total * each_mean, axis=0) / total_all)[:, None]
        student_lse = (top + jnp.log(total_all))[:, None]
        other_top = jnp.max(each_other, axis=0)
        other_all = jnp.sum(jnp.exp(each_other - other_top), axis=0)
        teacher_lse = (other_top + jnp.log(other_all))[:, None]
        divergence = mean - student_lse + teacher_lse
        log_student = student_logits - student_lse
        probs = jnp.exp(log_student)
        gap = log_student - (teacher_logits - teacher_lse)
        logit_grad = (probs * (gap - divergence)).astype(jnp.bfloat16)

        index = lax.axis_index("dp")
        half = logit_grad.shape[0] // 2
        keep, send = reorder([logit_grad[:half], logit_grad[half:]], index, core)
        away = jnp.dot(send, student_head, preferred_element_type=jnp.float32).astype(jnp.bfloat16)
        landed = swap(away, "dp", dp, 1)
        near = lax.optimization_barrier(
            jnp.dot(keep, student_head, preferred_element_type=jnp.float32)
        )
        acc = near + landed.astype(jnp.float32)
        head_grad = lax.dot_general(
            logit_grad, student_full, (((0,), (0,)), ((), ())), preferred_element_type=jnp.float32
        ).astype(jnp.bfloat16)
        acc = scattered(acc, "vocab", vocab, vocab_bits, 1)
        acc, head_grad = lax.optimization_barrier((acc, head_grad))
        acc = scattered(acc, "dp", dp, z_bits, 0, farthest_first=False)
        hidden_grad = acc.astype(jnp.bfloat16)
        return (hidden_grad, head_grad)

    return on_device


def solution(mesh):
    return jax.shard_map(
        build(mesh.shape["dp"], mesh.shape["vocab"]),
        mesh=mesh,
        in_specs=(
            P("dp", "vocab"),
            P("dp", "vocab"),
            P(("dp", "vocab"), None),
            P(("dp", "vocab"), None),
        ),
        out_specs=(P("dp", "vocab"), P(("dp", "vocab"), None)),
        check_vma=False,
    )
```

```python
import jax
import jax.numpy as jnp
from jax import lax
from jax.sharding import PartitionSpec as P


def grouped(bits):
    bits = list(bits)
    return [bits[i : i + 2] for i in range(0, len(bits), 2)]


def mask_of(j, bits):
    return sum(((j >> k) & 1) << bit for k, bit in enumerate(bits))


def reorder(parts, index, bits):
    for k, bit in enumerate(bits):
        lower = ((index >> bit) & 1) == 0
        parts = [jnp.where(lower, parts[j], parts[j ^ (1 << k)]) for j in range(len(parts))]
    return parts


def swap(value, axis, size, mask):
    return lax.ppermute(value, axis, [(i, i ^ mask) for i in range(size)])


def gathered(value, axis, size, bits, dim, first=3):
    index = lax.axis_index(axis)
    for group in grouped(bits):
        order = sorted(range(1, 1 << len(group)), key=lambda j: (j != first, -j))
        landed = [swap(value, axis, size, mask_of(j, group)) for j in order]
        landed = dict(zip(reversed(order), lax.optimization_barrier(landed[::-1])))
        parts = [landed[j] for j in sorted(order)]
        parts = [value] + parts
        value = jnp.concatenate(reorder(parts, index, group), axis=dim)
    return value


def scattered(total, axis, size, bits, dim):
    index = lax.axis_index(axis)
    for group in reversed(grouped(bits)):
        parts = reorder(jnp.split(total, 1 << len(group), axis=dim), index, group)
        total = parts[0]
        landed = [
            swap(parts[j].astype(jnp.bfloat16), axis, size, mask_of(j, group))
            for j in reversed(range(1, 1 << len(group)))
        ]
        for part in landed:
            total = total + part.astype(jnp.float32)
    return total


def build(dp, vocab):
    dp_bits = range(dp.bit_length() - 1)
    vocab_bits = range(vocab.bit_length() - 1)
    core, z_bits = dp_bits[:1], dp_bits[1:]

    def on_device(student_hidden, teacher_hidden, student_head, teacher_head):
        rows, share = student_hidden.shape
        teacher_share = teacher_hidden.shape[1]
        tokens = rows * dp
        lane = lax.broadcasted_iota(jnp.int32, (rows, share + teacher_share), 1)
        packed = jnp.where(
            lane < share,
            jnp.pad(student_hidden, ((0, 0), (0, teacher_share))),
            jnp.pad(teacher_hidden, ((0, 0), (share, 0))),
        )
        by_z = gathered(packed, "dp", dp, z_bits, 0, first=2)
        by_vocab = gathered(by_z[None], "vocab", vocab, vocab_bits, 0)
        whole = gathered(by_vocab, "dp", dp, core, 1)
        student_full = jnp.concatenate([whole[i, :, :share] for i in range(vocab)], axis=1)
        teacher_full = jnp.concatenate([whole[i, :, share:] for i in range(vocab)], axis=1)

        contract = (((1,), (1,)), ((), ()))
        student_logits = lax.dot_general(
            student_full, student_head, contract, preferred_element_type=jnp.float32
        )
        teacher_logits = lax.dot_general(
            teacher_full, teacher_head, contract, preferred_element_type=jnp.float32
        )
        peak = jnp.max(student_logits, axis=1)
        shifted = jnp.exp(student_logits - peak[:, None])
        total = jnp.sum(shifted, axis=1)
        weighted = jnp.sum(shifted * (student_logits - teacher_logits), axis=1)
        other_peak = jnp.max(teacher_logits, axis=1)
        other_total = jnp.sum(jnp.exp(teacher_logits - other_peak[:, None]), axis=1)
        lanes = -(-tokens // 64) * 64
        stats = jnp.stack([
            peak,
            total,
            weighted / total,
            other_peak + jnp.log(other_total),
        ])
        stats = jnp.pad(stats, ((0, 0), (0, lanes - tokens))).reshape(2, 2 * lanes)
        devices = dp * vocab
        every = lax.all_to_all(
            jnp.broadcast_to(stats[None], (devices,) + stats.shape),
            ("dp", "vocab"), 0, 0, tiled=True,
        )
        each_peak = every[:, 0, :tokens]
        each_total = every[:, 0, lanes : lanes + tokens]
        each_mean = every[:, 1, :tokens]
        each_other = every[:, 1, lanes : lanes + tokens]
        top = jnp.max(each_peak, axis=0)
        each_total = each_total * jnp.exp(each_peak - top)
        total_all = jnp.sum(each_total, axis=0)
        mean = (jnp.sum(each_total * each_mean, axis=0) / total_all)[:, None]
        student_lse = (top + jnp.log(total_all))[:, None]
        other_top = jnp.max(each_other, axis=0)
        other_all = jnp.sum(jnp.exp(each_other - other_top), axis=0)
        teacher_lse = (other_top + jnp.log(other_all))[:, None]
        divergence = mean - student_lse + teacher_lse
        log_student = student_logits - student_lse
        probs = jnp.exp(log_student)
        gap = log_student - (teacher_logits - teacher_lse)
        logit_grad = (probs * (gap - divergence)).astype(jnp.bfloat16)

        index = lax.axis_index("dp")
        half = logit_grad.shape[0] // 2
        keep, send = reorder([logit_grad[:half], logit_grad[half:]], index, core)
        away = jnp.dot(send, student_head, preferred_element_type=jnp.float32).astype(jnp.bfloat16)
        landed = swap(away, "dp", dp, 1)
        near = lax.optimization_barrier(
            jnp.dot(keep, student_head, preferred_element_type=jnp.float32)
        )
        acc = near + landed.astype(jnp.float32)
        head_grad = lax.dot_general(
            logit_grad, student_full, (((0,), (0,)), ((), ())), preferred_element_type=jnp.float32
        ).astype(jnp.bfloat16)
        acc = scattered(acc, "vocab", vocab, vocab_bits, 1)
        acc, head_grad = lax.optimization_barrier((acc, head_grad))
        acc = scattered(acc, "dp", dp, z_bits, 0)
        hidden_grad = acc.astype(jnp.bfloat16)
        return (hidden_grad, head_grad)

    return on_device


def solution(mesh):
    return jax.shard_map(
        build(mesh.shape["dp"], mesh.shape["vocab"]),
        mesh=mesh,
        in_specs=(
            P("dp", "vocab"),
            P("dp", "vocab"),
            P(("dp", "vocab"), None),
            P(("dp", "vocab"), None),
        ),
        out_specs=(P("dp", "vocab"), P(("dp", "vocab"), None)),
        check_vma=False,
    )
```

```python
import jax
import jax.numpy as jnp
from jax import lax
from jax.sharding import PartitionSpec as P


def grouped(bits):
    bits = list(bits)
    return [bits[i : i + 2] for i in range(0, len(bits), 2)]


def mask_of(j, bits):
    return sum(((j >> k) & 1) << bit for k, bit in enumerate(bits))


def reorder(parts, index, bits):
    for k, bit in enumerate(bits):
        lower = ((index >> bit) & 1) == 0
        parts = [jnp.where(lower, parts[j], parts[j ^ (1 << k)]) for j in range(len(parts))]
    return parts


def swap(value, axis, size, mask):
    return lax.ppermute(value, axis, [(i, i ^ mask) for i in range(size)])


def gathered(value, axis, size, bits, dim):
    index = lax.axis_index(axis)
    for group in grouped(bits):
        landed = {
            j: swap(value, axis, size, mask_of(j, group))
            for j in reversed(range(1, 1 << len(group)))
        }
        parts = lax.optimization_barrier([landed[j] for j in range(1, 1 << len(group))])
        parts = [value] + list(parts)
        value = jnp.concatenate(reorder(parts, index, group), axis=dim)
    return value


def scattered(total, axis, size, bits, dim):
    index = lax.axis_index(axis)
    for group in reversed(grouped(bits)):
        parts = reorder(jnp.split(total, 1 << len(group), axis=dim), index, group)
        total = parts[0]
        landed = [
            swap(parts[j].astype(jnp.bfloat16), axis, size, mask_of(j, group))
            for j in reversed(range(1, 1 << len(group)))
        ]
        for part in landed:
            total = total + part.astype(jnp.float32)
    return total


def scattered_mixed(total, axis, size, bits, dim):
    index = lax.axis_index(axis)
    for group in reversed(grouped(bits)):
        parts = reorder(jnp.split(total, 1 << len(group), axis=dim), index, group)
        total = parts[0]
        parts = [part.astype(jnp.bfloat16) for part in parts]
        if len(group) == 2:
            bit = group[1]
            upper = ((index >> bit) & 1) == 1
            near, second, far = [mask_of(j, group) for j in (1, 2, 3)]
            one = jnp.where(upper, parts[2], parts[3])
            other = jnp.where(upper, parts[3], parts[2])
            one, other, last = lax.optimization_barrier((one, other, parts[1]))
            landed = [
                lax.ppermute(one, axis, [
                    (i, i ^ (second if (i >> bit) & 1 else far)) for i in range(size)
                ]),
                lax.ppermute(other, axis, [
                    (i, i ^ (far if (i >> bit) & 1 else second)) for i in range(size)
                ]),
                swap(last, axis, size, near),
            ]
        else:
            landed = [swap(parts[1], axis, size, mask_of(1, group))]
        for part in landed:
            total = total + part.astype(jnp.float32)
    return total


def build(dp, vocab):
    dp_bits = range(dp.bit_length() - 1)
    vocab_bits = range(vocab.bit_length() - 1)
    core, z_bits = dp_bits[:1], dp_bits[1:]

    def on_device(student_hidden, teacher_hidden, student_head, teacher_head):
        rows, share = student_hidden.shape
        teacher_share = teacher_hidden.shape[1]
        tokens = rows * dp
        lane = lax.broadcasted_iota(jnp.int32, (rows, share + teacher_share), 1)
        packed = jnp.where(
            lane < share,
            jnp.pad(student_hidden, ((0, 0), (0, teacher_share))),
            jnp.pad(teacher_hidden, ((0, 0), (share, 0))),
        )
        by_z = gathered(packed, "dp", dp, z_bits, 0)
        by_vocab = gathered(by_z[None], "vocab", vocab, vocab_bits, 0)
        whole = gathered(by_vocab, "dp", dp, core, 1)
        student_full = jnp.concatenate([whole[i, :, :share] for i in range(vocab)], axis=1)
        teacher_full = jnp.concatenate([whole[i, :, share:] for i in range(vocab)], axis=1)

        contract = (((1,), (1,)), ((), ()))
        student_logits = lax.dot_general(
            student_full, student_head, contract, preferred_element_type=jnp.float32
        )
        teacher_logits = lax.dot_general(
            teacher_full, teacher_head, contract, preferred_element_type=jnp.float32
        )
        peak = jnp.max(student_logits, axis=1)
        shifted = jnp.exp(student_logits - peak[:, None])
        total = jnp.sum(shifted, axis=1)
        weighted = jnp.sum(shifted * (student_logits - teacher_logits), axis=1)
        other_peak = jnp.max(teacher_logits, axis=1)
        other_total = jnp.sum(jnp.exp(teacher_logits - other_peak[:, None]), axis=1)
        lanes = -(-tokens // 64) * 64
        stats = jnp.stack([
            peak,
            total,
            weighted / total,
            other_peak + jnp.log(other_total),
        ])
        stats = jnp.pad(stats, ((0, 0), (0, lanes - tokens))).reshape(2, 2 * lanes)
        devices = dp * vocab
        every = lax.all_to_all(
            jnp.broadcast_to(stats[None], (devices,) + stats.shape),
            ("dp", "vocab"), 0, 0, tiled=True,
        )
        each_peak = every[:, 0, :tokens]
        each_total = every[:, 0, lanes : lanes + tokens]
        each_mean = every[:, 1, :tokens]
        each_other = every[:, 1, lanes : lanes + tokens]
        top = jnp.max(each_peak, axis=0)
        each_total = each_total * jnp.exp(each_peak - top)
        total_all = jnp.sum(each_total, axis=0)
        mean = (jnp.sum(each_total * each_mean, axis=0) / total_all)[:, None]
        student_lse = (top + jnp.log(total_all))[:, None]
        other_top = jnp.max(each_other, axis=0)
        other_all = jnp.sum(jnp.exp(each_other - other_top), axis=0)
        teacher_lse = (other_top + jnp.log(other_all))[:, None]
        divergence = mean - student_lse + teacher_lse
        log_student = student_logits - student_lse
        probs = jnp.exp(log_student)
        gap = log_student - (teacher_logits - teacher_lse)
        logit_grad = (probs * (gap - divergence)).astype(jnp.bfloat16)

        index = lax.axis_index("dp")
        half = logit_grad.shape[0] // 2
        keep, send = reorder([logit_grad[:half], logit_grad[half:]], index, core)
        away = jnp.dot(send, student_head, preferred_element_type=jnp.float32).astype(jnp.bfloat16)
        landed = swap(away, "dp", dp, 1)
        near = lax.optimization_barrier(
            jnp.dot(keep, student_head, preferred_element_type=jnp.float32)
        )
        acc = near + landed.astype(jnp.float32)
        head_grad = lax.dot_general(
            logit_grad, student_full, (((0,), (0,)), ((), ())), preferred_element_type=jnp.float32
        ).astype(jnp.bfloat16)
        acc = scattered(acc, "vocab", vocab, vocab_bits, 1)
        acc, head_grad = lax.optimization_barrier((acc, head_grad))
        acc = scattered_mixed(acc, "dp", dp, z_bits, 0)
        hidden_grad = acc.astype(jnp.bfloat16)
        return (hidden_grad, head_grad)

    return on_device


def solution(mesh):
    return jax.shard_map(
        build(mesh.shape["dp"], mesh.shape["vocab"]),
        mesh=mesh,
        in_specs=(
            P("dp", "vocab"),
            P("dp", "vocab"),
            P(("dp", "vocab"), None),
            P(("dp", "vocab"), None),
        ),
        out_specs=(P("dp", "vocab"), P(("dp", "vocab"), None)),
        check_vma=False,
    )
```

```python
import jax
import jax.numpy as jnp
from jax import lax
from jax.experimental import pallas as pl
from jax.experimental.pallas import tpu as pltpu
from jax.sharding import PartitionSpec as P


def grouped(bits):
    bits = list(bits)
    return [bits[i : i + 2] for i in range(0, len(bits), 2)]


def mask_of(j, bits):
    return sum(((j >> k) & 1) << bit for k, bit in enumerate(bits))


def reorder(parts, index, bits):
    for k, bit in enumerate(bits):
        lower = ((index >> bit) & 1) == 0
        parts = [jnp.where(lower, parts[j], parts[j ^ (1 << k)]) for j in range(len(parts))]
    return parts


def swap(value, axis, size, mask):
    return lax.ppermute(value, axis, [(i, i ^ mask) for i in range(size)])


def gathered(value, axis, size, bits, dim):
    index = lax.axis_index(axis)
    for group in grouped(bits):
        landed = {
            j: swap(value, axis, size, mask_of(j, group))
            for j in reversed(range(1, 1 << len(group)))
        }
        parts = lax.optimization_barrier([landed[j] for j in range(1, 1 << len(group))])
        parts = [value] + list(parts)
        value = jnp.concatenate(reorder(parts, index, group), axis=dim)
    return value


def scattered(total, axis, size, bits, dim):
    index = lax.axis_index(axis)
    for group in reversed(grouped(bits)):
        parts = reorder(jnp.split(total, 1 << len(group), axis=dim), index, group)
        total = parts[0]
        landed = [
            swap(parts[j].astype(jnp.bfloat16), axis, size, mask_of(j, group))
            for j in reversed(range(1, 1 << len(group)))
        ]
        for part in landed:
            total = total + part.astype(jnp.float32)
    return total


def side_by_side(left, right):
    rows, width = left.shape[0], left.shape[1] + right.shape[1]
    if left.shape[1] % 128:
        return jnp.concatenate([left, right], axis=1)

    def kernel(left_ref, right_ref, out_ref, sems):
        copies = [
            pltpu.make_async_copy(left_ref, out_ref.at[:, : left.shape[1]], sems.at[0]),
            pltpu.make_async_copy(right_ref, out_ref.at[:, left.shape[1] :], sems.at[1]),
        ]
        for copy in copies:
            copy.start()
        for copy in copies:
            copy.wait()

    return pl.pallas_call(
        kernel,
        out_shape=jax.ShapeDtypeStruct((rows, width), left.dtype),
        in_specs=[pl.BlockSpec(memory_space=pltpu.HBM)] * 2,
        out_specs=pl.BlockSpec(memory_space=pltpu.VMEM),
        scratch_shapes=[pltpu.SemaphoreType.DMA((2,))],
        cost_estimate=pl.CostEstimate(
            flops=0, bytes_accessed=4 * rows * width, transcendentals=0
        ),
    )(left, right)


def build(dp, vocab):
    dp_bits = range(dp.bit_length() - 1)
    vocab_bits = range(vocab.bit_length() - 1)
    core, z_bits = dp_bits[:1], dp_bits[1:]

    def on_device(student_hidden, teacher_hidden, student_head, teacher_head):
        rows, share = student_hidden.shape
        teacher_share = teacher_hidden.shape[1]
        tokens = rows * dp
        packed = side_by_side(student_hidden, teacher_hidden)
        by_z = gathered(packed, "dp", dp, z_bits, 0)
        by_vocab = gathered(by_z[None], "vocab", vocab, vocab_bits, 0)
        whole = gathered(by_vocab, "dp", dp, core, 1)
        student_full = jnp.concatenate([whole[i, :, :share] for i in range(vocab)], axis=1)
        teacher_full = jnp.concatenate([whole[i, :, share:] for i in range(vocab)], axis=1)

        contract = (((1,), (1,)), ((), ()))
        student_logits = lax.dot_general(
            student_full, student_head, contract, preferred_element_type=jnp.float32
        )
        teacher_logits = lax.dot_general(
            teacher_full, teacher_head, contract, preferred_element_type=jnp.float32
        )
        peak = jnp.max(student_logits, axis=1)
        shifted = jnp.exp(student_logits - peak[:, None])
        total = jnp.sum(shifted, axis=1)
        weighted = jnp.sum(shifted * (student_logits - teacher_logits), axis=1)
        other_peak = jnp.max(teacher_logits, axis=1)
        other_total = jnp.sum(jnp.exp(teacher_logits - other_peak[:, None]), axis=1)
        lanes = -(-tokens // 64) * 64
        stats = jnp.stack([
            peak,
            total,
            weighted / total,
            other_peak + jnp.log(other_total),
        ])
        stats = jnp.pad(stats, ((0, 0), (0, lanes - tokens))).reshape(2, 2 * lanes)
        devices = dp * vocab
        every = lax.all_to_all(
            jnp.broadcast_to(stats[None], (devices,) + stats.shape),
            ("dp", "vocab"), 0, 0, tiled=True,
        )
        each_peak = every[:, 0, :tokens]
        each_total = every[:, 0, lanes : lanes + tokens]
        each_mean = every[:, 1, :tokens]
        each_other = every[:, 1, lanes : lanes + tokens]
        top = jnp.max(each_peak, axis=0)
        each_total = each_total * jnp.exp(each_peak - top)
        total_all = jnp.sum(each_total, axis=0)
        mean = (jnp.sum(each_total * each_mean, axis=0) / total_all)[:, None]
        student_lse = (top + jnp.log(total_all))[:, None]
        other_top = jnp.max(each_other, axis=0)
        other_all = jnp.sum(jnp.exp(each_other - other_top), axis=0)
        teacher_lse = (other_top + jnp.log(other_all))[:, None]
        divergence = mean - student_lse + teacher_lse
        log_student = student_logits - student_lse
        probs = jnp.exp(log_student)
        gap = log_student - (teacher_logits - teacher_lse)
        logit_grad = (probs * (gap - divergence)).astype(jnp.bfloat16)

        index = lax.axis_index("dp")
        half = logit_grad.shape[0] // 2
        keep, send = reorder([logit_grad[:half], logit_grad[half:]], index, core)
        away = jnp.dot(send, student_head, preferred_element_type=jnp.float32).astype(jnp.bfloat16)
        landed = swap(away, "dp", dp, 1)
        near = lax.optimization_barrier(
            jnp.dot(keep, student_head, preferred_element_type=jnp.float32)
        )
        acc = near + landed.astype(jnp.float32)
        head_grad = lax.dot_general(
            logit_grad, student_full, (((0,), (0,)), ((), ())), preferred_element_type=jnp.float32
        ).astype(jnp.bfloat16)
        acc = scattered(acc, "vocab", vocab, vocab_bits, 1)
        acc, head_grad = lax.optimization_barrier((acc, head_grad))
        acc = scattered(acc, "dp", dp, z_bits, 0)
        hidden_grad = acc.astype(jnp.bfloat16)
        return (hidden_grad, head_grad)

    return on_device


def solution(mesh):
    return jax.shard_map(
        build(mesh.shape["dp"], mesh.shape["vocab"]),
        mesh=mesh,
        in_specs=(
            P("dp", "vocab"),
            P("dp", "vocab"),
            P(("dp", "vocab"), None),
            P(("dp", "vocab"), None),
        ),
        out_specs=(P("dp", "vocab"), P(("dp", "vocab"), None)),
        check_vma=False,
    )
```

```python
import jax
import jax.numpy as jnp
from jax import lax
from jax.sharding import PartitionSpec as P


def grouped(bits):
    bits = list(bits)
    return [bits[i : i + 2] for i in range(0, len(bits), 2)]


def mask_of(j, bits):
    return sum(((j >> k) & 1) << bit for k, bit in enumerate(bits))


def reorder(parts, index, bits):
    for k, bit in enumerate(bits):
        lower = ((index >> bit) & 1) == 0
        parts = [jnp.where(lower, parts[j], parts[j ^ (1 << k)]) for j in range(len(parts))]
    return parts


def swap(value, axis, size, mask):
    return lax.ppermute(value, axis, [(i, i ^ mask) for i in range(size)])


def gathered(value, axis, size, bits, dim):
    index = lax.axis_index(axis)
    for group in grouped(bits):
        landed = {
            j: swap(value, axis, size, mask_of(j, group))
            for j in reversed(range(1, 1 << len(group)))
        }
        order = sorted(landed, key=lambda j: (j == 3, -j if axis == "vocab" else j))
        landed = dict(zip(order, lax.optimization_barrier([landed[j] for j in order])))
        parts = [value] + [landed[j] for j in sorted(order)]
        value = jnp.concatenate(reorder(parts, index, group), axis=dim)
    return value


def scattered(total, axis, size, bits, dim):
    index = lax.axis_index(axis)
    for group in reversed(grouped(bits)):
        parts = reorder(jnp.split(total, 1 << len(group), axis=dim), index, group)
        total = parts[0]
        landed = [
            swap(parts[j].astype(jnp.bfloat16), axis, size, mask_of(j, group))
            for j in reversed(range(1, 1 << len(group)))
        ]
        for part in landed:
            total = total + part.astype(jnp.float32)
    return total


def build(dp, vocab):
    dp_bits = range(dp.bit_length() - 1)
    vocab_bits = range(vocab.bit_length() - 1)
    core, z_bits = dp_bits[:1], dp_bits[1:]

    def on_device(student_hidden, teacher_hidden, student_head, teacher_head):
        rows, share = student_hidden.shape
        teacher_share = teacher_hidden.shape[1]
        tokens = rows * dp
        lane = lax.broadcasted_iota(jnp.int32, (rows, share + teacher_share), 1)
        packed = jnp.where(
            lane < share,
            jnp.pad(student_hidden, ((0, 0), (0, teacher_share))),
            jnp.pad(teacher_hidden, ((0, 0), (share, 0))),
        )
        by_z = gathered(packed, "dp", dp, z_bits, 0)
        by_vocab = gathered(by_z[None], "vocab", vocab, vocab_bits, 0)
        whole = gathered(by_vocab, "dp", dp, core, 1)
        student_full = jnp.concatenate([whole[i, :, :share] for i in range(vocab)], axis=1)
        teacher_full = jnp.concatenate([whole[i, :, share:] for i in range(vocab)], axis=1)

        contract = (((1,), (1,)), ((), ()))
        student_logits = lax.dot_general(
            student_full, student_head, contract, preferred_element_type=jnp.float32
        )
        teacher_logits = lax.dot_general(
            teacher_full, teacher_head, contract, preferred_element_type=jnp.float32
        )
        peak = jnp.max(student_logits, axis=1)
        shifted = jnp.exp(student_logits - peak[:, None])
        total = jnp.sum(shifted, axis=1)
        weighted = jnp.sum(shifted * (student_logits - teacher_logits), axis=1)
        other_peak = jnp.max(teacher_logits, axis=1)
        other_total = jnp.sum(jnp.exp(teacher_logits - other_peak[:, None]), axis=1)
        lanes = -(-tokens // 64) * 64
        stats = jnp.stack([
            peak,
            total,
            weighted / total,
            other_peak + jnp.log(other_total),
        ])
        stats = jnp.pad(stats, ((0, 0), (0, lanes - tokens))).reshape(2, 2 * lanes)
        devices = dp * vocab
        every = lax.all_to_all(
            jnp.broadcast_to(stats[None], (devices,) + stats.shape),
            ("dp", "vocab"), 0, 0, tiled=True,
        )
        each_peak = every[:, 0, :tokens]
        each_total = every[:, 0, lanes : lanes + tokens]
        each_mean = every[:, 1, :tokens]
        each_other = every[:, 1, lanes : lanes + tokens]
        top = jnp.max(each_peak, axis=0)
        each_total = each_total * jnp.exp(each_peak - top)
        total_all = jnp.sum(each_total, axis=0)
        mean = (jnp.sum(each_total * each_mean, axis=0) / total_all)[:, None]
        student_lse = (top + jnp.log(total_all))[:, None]
        other_top = jnp.max(each_other, axis=0)
        other_all = jnp.sum(jnp.exp(each_other - other_top), axis=0)
        teacher_lse = (other_top + jnp.log(other_all))[:, None]
        divergence = mean - student_lse + teacher_lse
        log_student = student_logits - student_lse
        probs = jnp.exp(log_student)
        gap = log_student - (teacher_logits - teacher_lse)
        logit_grad = (probs * (gap - divergence)).astype(jnp.bfloat16)

        index = lax.axis_index("dp")
        half = logit_grad.shape[0] // 2
        keep, send = reorder([logit_grad[:half], logit_grad[half:]], index, core)
        away = jnp.dot(send, student_head, preferred_element_type=jnp.float32).astype(jnp.bfloat16)
        landed = swap(away, "dp", dp, 1)
        near = lax.optimization_barrier(
            jnp.dot(keep, student_head, preferred_element_type=jnp.float32)
        )
        acc = near + landed.astype(jnp.float32)
        head_grad = lax.dot_general(
            logit_grad, student_full, (((0,), (0,)), ((), ())), preferred_element_type=jnp.float32
        ).astype(jnp.bfloat16)
        acc = scattered(acc, "vocab", vocab, vocab_bits, 1)
        acc, head_grad = lax.optimization_barrier((acc, head_grad))
        acc = scattered(acc, "dp", dp, z_bits, 0)
        hidden_grad = acc.astype(jnp.bfloat16)
        return (hidden_grad, head_grad)

    return on_device


def solution(mesh):
    return jax.shard_map(
        build(mesh.shape["dp"], mesh.shape["vocab"]),
        mesh=mesh,
        in_specs=(
            P("dp", "vocab"),
            P("dp", "vocab"),
            P(("dp", "vocab"), None),
            P(("dp", "vocab"), None),
        ),
        out_specs=(P("dp", "vocab"), P(("dp", "vocab"), None)),
        check_vma=False,
    )
```
